32 devices in a mesh: sec: 4 (over x, core), term: 8 (over z, y).
Axes of the slice: x: 2, y: 2, z: 4, core: 2. Of those that a mesh axis runs over, the one named last changes fastest.
Arguments:
- env_blocks: bfloat16 [8, 8, 256, 256], P('term', 'sec'), may hold values from -6 to 6
- core_blocks: bfloat16 [256, 256, 256], P('sec', 'term'), may hold values from -0.375 to 0.375
- mpo_coeffs: bfloat16 [8, 8, 256], P(None, None, 'sec'), may hold values from -2 to 2
- pair_left: int32 [256], P('sec'), may hold values from 0 to 1
- pair_right: int32 [256], P('sec'), may hold values from 0 to 7
- block_dims: int32 [8], replicated, may hold values from 1 to 256, 1536 in all
Outputs:
- new_env: float32 [8, 8, 256, 256], P('term', 'sec')
The draws below stay inside these ranges and needn't reach their ends.
Inputs may be any that keep to these rules, and one draw needn't show every extreme that they name: `pair_left`: A pair's left block is one of the 2 blocks of the sec index that holds the pair.
All inputs are finite; a program needn't handle non-finite values.
Results may differ from the reference program's by a relative error of at most 0.004.
Values may be sent and summed in bfloat16 or wider, within the bound.
No kernel may reach another device: no remote copies, remote signals or barrier semaphores. Data moves between devices by JAX's collectives and lax.ppermute only.
A program may use at most 128 MiB of HBM per device.

```python
import math
import jax
import jax.numpy as jnp
import numpy as np
from jax import lax

BLK = 256
NB_DEV = 2
PAIR_DEV = 64
NB = 8
PAIRS = 256
W = 8


def touch_ends(entries, rng, low, high):
    place = [jax.random.randint(jax.random.fold_in(rng, axis), (), 0, length) for axis, length in enumerate(entries.shape)]
    main_axis = entries.shape.index(max(entries.shape))
    next_to = place[:main_axis] + [(place[main_axis] + 1) % entries.shape[main_axis]] + place[main_axis + 1:]
    return entries.at[tuple(place)].set(low).at[tuple(next_to)].set(high)


def shard_levels(own_key, shape, split, smallest, high):
    def one(position, parts):
        heights = jax.random.uniform(jax.random.fold_in(jax.random.fold_in(own_key, 6), position), (parts,), jnp.float32, smallest / len(split), high / len(split))
        return jnp.repeat(jnp.exp(heights), shape[position] // parts).reshape((-1,) + (1,) * (len(shape) - position - 1))

    gain = one(*split[0])
    for cut in split[1:]:
        gain = gain * one(*cut)
    return gain


def length_profile(count, total, most, lean):
    weights = [(1 << 20) // math.isqrt(grade ** lean) + 1 for grade in range(2, count + 1)]
    rest, holding = total - most - (count - 1), [1] * (count - 1)
    while rest > 0:
        movable = [i for i in range(count - 1) if holding[i] < most]
        pool, budget = sum([weights[i] for i in movable]), rest
        for i in movable:
            more = min(most - holding[i], max(1, budget * weights[i] // pool), rest)
            holding[i] = holding[i] + more
            rest = rest - more
    return np.array([most] + holding)


def ragged(stream_key, number_of, total, limit, skew):
    if number_of == 2:
        one = jax.random.randint(stream_key, (), max(1, total - limit), min(limit, total - 1) + 1)
        return jnp.stack([one, total - one])
    tallies = jnp.asarray(length_profile(number_of, total, limit, skew), jnp.int32)
    couples = (number_of - 1) // 2
    giver, sink = tallies[1:1 + 2 * couples:2], tallies[2:2 + 2 * couples:2]
    slack = jnp.minimum(giver - 1, limit - sink)
    shifted = jax.random.randint(jax.random.fold_in(stream_key, 1), (couples,), 0, 1 << 20) % (slack + 1)
    tallies = tallies.at[1:1 + 2 * couples:2].set(giver - shifted).at[2:2 + 2 * couples:2].set(sink + shifted)
    return tallies[jax.random.permutation(jax.random.fold_in(stream_key, 2), number_of)]


def normal_values(stream_key, dims, spread, limit, shards=(), held_as=jnp.bfloat16):
    values = spread * jax.random.normal(stream_key, dims, jnp.float32)
    if shards:
        values = values * shard_levels(stream_key, dims, shards, -0.22, 0.18)
    return jnp.clip(values, -limit, limit).astype(held_as)


def setup_inputs(seed: int = 0) -> dict:
    key_of = jax.random.split(jax.random.key(seed), 7)
    env_blocks = normal_values(key_of[0], (W, NB, BLK, BLK), 1.0, 6.0, ((0, 8), (1, 4)))
    core_blocks = normal_values(key_of[1], (PAIRS, BLK, BLK), BLK ** -0.5, 0.375, ((0, 4), (1, 8)))
    mpo_coeffs = normal_values(key_of[2], (W, W, PAIRS), W ** -0.5, 2.0, ((2, 4),))
    pair_left = touch_ends(jax.random.randint(key_of[3], (PAIRS,), 0, NB_DEV), jax.random.fold_in(key_of[3], 1), 0, NB_DEV - 1).astype(jnp.int32)
    pair_right = touch_ends(jax.random.randint(key_of[4], (PAIRS,), 0, NB), jax.random.fold_in(key_of[4], 1), 0, NB - 1).astype(jnp.int32)
    block_dims = ragged(key_of[5], NB, NB * BLK * 3 // 4, BLK, 0).astype(jnp.int32)
    return {"env_blocks": env_blocks, "core_blocks": core_blocks, "mpo_coeffs": mpo_coeffs, "pair_left": pair_left, "pair_right": pair_right, "block_dims": block_dims}


def reference(env_blocks, core_blocks, mpo_coeffs, pair_left, pair_right, block_dims):
    rows = jnp.arange(BLK).astype(jnp.int32)
    left_all = ((jnp.arange(PAIRS).astype(jnp.int32) // PAIR_DEV) * NB_DEV + pair_left).astype(jnp.int32)
    coeff_pairs = jnp.moveaxis(mpo_coeffs, 2, 0)

    def one_pair(carry, items):
        core, left_block, right_block, coeff = items
        dim_left = block_dims[left_block]
        dim_right = block_dims[right_block]
        keep = (rows < dim_left)[:, None] & (rows < dim_right)[None, :]
        masked = jnp.where(keep, core, jnp.zeros((), core.dtype))
        envs = lax.dynamic_index_in_dim(env_blocks, left_block, 1, keepdims=False)
        mixed = jnp.einsum('wv,wrc->vrc', coeff.astype(jnp.float32), envs.astype(jnp.float32)).astype(jnp.bfloat16)
        half = jnp.einsum('vrc,cd->vrd', mixed.astype(jnp.float32), masked.astype(jnp.float32)).astype(jnp.bfloat16)
        term = jnp.einsum('rc,vrd->vcd', masked.astype(jnp.float32), half.astype(jnp.float32))
        carry = carry.at[:, right_block].add(term)
        return carry, None

    start = jnp.zeros((W, NB, BLK, BLK), jnp.float32)
    result, _ = lax.scan(one_pair, start, (core_blocks, left_all, pair_right, coeff_pairs))
    return result
```

```python
import functools

import jax
import jax.numpy as jnp
from jax import lax
from jax.experimental import pallas as pl
from jax.experimental.pallas import tpu as pltpu
from jax.sharding import PartitionSpec as P

BF16, F32 = jnp.bfloat16, jnp.float32
TILE = 16


def pair_kernel(plan, pieces, groups, slots, *refs):
    place, info, mix = refs[:3]
    piece_refs = refs[3 : 3 + pieces]
    keep_ref = refs[3 + pieces]
    send_refs = refs[4 + pieces : 4 + pieces + groups - 1]
    core, env, mixed, total, sems = refs[4 + pieces + groups - 1 :]
    pairs, blk = core.shape[0], core.shape[1]
    env_copies, core_copies = [], []
    sem = 0
    for n, (core_first, core_count, env_first, env_count) in enumerate(plan):
        ref = piece_refs[n]
        rows = ref.shape[1]
        if env_count:
            for part in range(rows // TILE):
                at = pl.multiple_of(place[2, n] * TILE, TILE)
                copy = pltpu.make_async_copy(
                    ref.at[pl.ds(env_first, env_count), pl.ds(part * TILE, TILE), :],
                    env.at[:, part, pl.ds(at, TILE), :],
                    sems.at[sem],
                )
                sem += 1
                copy.start()
                env_copies.append(copy)
    for n, (core_first, core_count, env_first, env_count) in enumerate(plan):
        ref = piece_refs[n]
        rows = ref.shape[1]
        if core_count:
            at = pl.multiple_of(place[0, n], rows)
            copy = pltpu.make_async_copy(
                ref.at[pl.ds(core_first, core_count), :, :],
                core.at[pl.ds(place[1, n], core_count), pl.ds(at, rows), :],
                sems.at[sem],
            )
            sem += 1
            copy.start()
            core_copies.append(copy)
    total[...] = jnp.zeros_like(total)
    for copy in env_copies:
        copy.wait()
    parts = env.shape[1]

    def mix_rows(step, carry):
        rows = jnp.dot(mix[...], env[step // parts, step % parts], preferred_element_type=F32)
        at = pl.multiple_of(step * TILE, TILE)
        mixed[:, pl.ds(at, TILE), :] = rows.astype(BF16).reshape(pairs, TILE, blk)
        return carry

    lax.fori_loop(0, blk // TILE, mix_rows, 0, unroll=2)
    for copy in core_copies:
        copy.wait()
    row = lax.broadcasted_iota(jnp.int32, (blk, blk), 0)
    col = lax.broadcasted_iota(jnp.int32, (blk, blk), 1)

    def one_pair(p, carry):
        keep = (row < info[0, p]) & (col < info[1, p])
        masked = jnp.where(keep, core[p].astype(F32), 0.0).astype(BF16)
        half = jnp.dot(mixed[p], masked, preferred_element_type=F32).astype(BF16)
        term = lax.dot_general(
            masked, half, (((0,), (0,)), ((), ())), preferred_element_type=F32
        )
        total[info[2, p]] += term
        return carry

    lax.fori_loop(0, pairs, one_pair, 0, unroll=4)
    keep_ref[...] = total[:slots]
    for f, ref in enumerate(send_refs):
        ref[...] = total[(f + 1) * slots : (f + 2) * slots].astype(BF16)


def pair_sums(plan, place, info, mix, pieces, groups, slots, env_rows):
    pairs = info.shape[1]
    blk = pieces[0].shape[2]
    rows = pieces[0].shape[1]
    copies = sum((1 if c[1] else 0) + (rows // TILE if c[3] else 0) for c in plan)
    smem = pl.BlockSpec(memory_space=pltpu.SMEM)
    vmem = pl.BlockSpec(memory_space=pltpu.VMEM)
    hbm = pl.BlockSpec(memory_space=pl.ANY)
    macs = 3 * pairs * blk * blk * blk
    return pl.pallas_call(
        functools.partial(pair_kernel, plan, len(pieces), groups, slots),
        out_shape=[jax.ShapeDtypeStruct((slots, blk, blk), F32)]
        + [jax.ShapeDtypeStruct((slots, blk, blk), BF16)] * (groups - 1),
        in_specs=[smem, smem, vmem] + [hbm] * len(pieces),
        out_specs=[vmem] * groups,
        scratch_shapes=[
            pltpu.VMEM((pairs, blk, blk), BF16),
            pltpu.VMEM((blk // rows, rows // TILE, env_rows * TILE, blk), BF16),
            pltpu.VMEM((pairs, blk, blk), BF16),
            pltpu.VMEM((groups * slots, blk, blk), F32),
            pltpu.SemaphoreType.DMA((copies,)),
        ],
        compiler_params=pltpu.CompilerParams(vmem_limit_bytes=48 << 20),
        cost_estimate=pl.CostEstimate(flops=2 * macs, bytes_accessed=8 << 20, transcendentals=0),
        name="pair_sums",
    )(place, info, mix, *pieces)


def per_device(secs, terms, env_blocks, core_blocks, mpo_coeffs, pair_left, pair_right, block_dims):
    nx, nz = secs // 2, terms // 2
    half_z = nz // 2
    nb, blk = env_blocks.shape[1], env_blocks.shape[2]
    pairs_local, rows = core_blocks.shape[0], core_blocks.shape[1]
    piece_pairs = pairs_local // nz
    own_nb = nb // 2
    sec, term = lax.axis_index("sec"), lax.axis_index("term")
    x, c, z, y = sec // 2, sec % 2, term // 2, term % 2
    top, rest = z // half_z, z % half_z

    def send(value, to):
        perm = []
        for s in range(secs):
            for t in range(terms):
                d = to(s // 2, s % 2, t // 2, t % 2)
                if d is not None:
                    perm.append((s * terms + t, (d[0] * 2 + d[1]) * terms + d[2] * 2 + d[3]))
        return lax.ppermute(value, ("sec", "term"), perm)

    def other_core(value):
        return send(value, lambda x, c, z, y: (x, 1 - c, z, y))

    facts = jnp.concatenate(
        [
            mpo_coeffs.reshape(-1, pairs_local).astype(F32),
            pair_left[None].astype(F32),
            pair_right[None].astype(F32),
        ]
    )
    facts = jnp.where(c == top, facts, other_core(facts))
    facts = lax.dynamic_slice_in_dim(facts, rest * 2 * piece_pairs, 2 * piece_pairs, 1)
    left, right = facts[-2].astype(jnp.int32), facts[-1].astype(jnp.int32)
    coeffs = facts[:-2].reshape(mpo_coeffs.shape[0], mpo_coeffs.shape[1], -1).astype(BF16)
    left_block = (x * 2 + top) * nb + left
    ids = jnp.arange(block_dims.shape[0])
    dims_left = jnp.sum(jnp.where(left_block[:, None] == ids, block_dims, 0), axis=1)
    dims_right = jnp.sum(jnp.where(right[:, None] == ids, block_dims, 0), axis=1)
    slots = 2 * nb
    slot = ((right // slots) ^ x) * slots + right % slots
    info = jnp.stack([dims_left, dims_right, slot])

    blocks = env_blocks[0].reshape(2, own_nb * (blk // rows), rows, blk)
    pieces, places = [], []
    zm = []
    for m in range(nz):
        g = z ^ m
        own = lax.dynamic_slice_in_dim(core_blocks, g * piece_pairs, piece_pairs, 0)
        message = jnp.concatenate([own, lax.dynamic_index_in_dim(blocks, g % 2, 0, keepdims=False)])
        zm.append(
            send(
                message,
                lambda x, c, z, y, m=m: (x, (z ^ m) % 2, c * half_z + (z ^ m) // 2, y),
            )
        )
    for m in range(nz):
        ym = send(zm[m], lambda x, c, z, y: (x, c, z, 1 - y))
        for k, got in ((c, (zm[m], ym)), (1 - c, (other_core(zm[m]), other_core(ym)))):
            from_z = (2 * rest + k) ^ m
            for from_y, value in zip((y, 1 - y), got):
                pieces.append(value)
                from_term = 2 * from_z + from_y
                places.append((from_term * rows, k * piece_pairs, from_term * nb + k * own_nb))
    place = jnp.stack([jnp.stack(p) for p in zip(*places)])
    env_rows = mpo_coeffs.shape[0] * nb
    if rows % TILE == 0 and own_nb == 1:
        plan = [(0, piece_pairs, piece_pairs, blk // rows)] * len(pieces)
    else:
        cores = jnp.zeros((2 * piece_pairs, blk, blk), BF16)
        envs = jnp.zeros((env_rows, blk, blk), BF16)
        for value, (at, first, which) in zip(pieces, places):
            cores = lax.dynamic_update_slice(cores, value[:piece_pairs], (first, at, 0))
            envs = lax.dynamic_update_slice(
                envs, value[piece_pairs:].reshape(own_nb, blk, blk), (which, 0, 0)
            )
        pieces = [cores] + [envs[n : n + 1] for n in range(env_rows)]
        plan = [(0, 2 * piece_pairs, 0, 0)] + [(0, 0, 0, 1)] * env_rows
        zero = jnp.zeros((1 + env_rows,), jnp.int32)
        place = jnp.stack([zero, zero, jnp.maximum(jnp.arange(1 + env_rows) - 1, 0)])

    onehot = (left[:, None] == jnp.arange(nb)).astype(BF16)
    eye = jnp.eye(TILE, dtype=BF16)

    def partial_sums(e):
        v = 2 * (c * half_z + (rest ^ e)) + y
        own = lax.dynamic_index_in_dim(coeffs, v, 1, keepdims=False)
        weights = own.T[:, :, None] * onehot[:, None, :]
        mix = weights.reshape(-1, 1, env_rows, 1) * eye[None, :, None, :]
        mix = mix.reshape(-1, env_rows * TILE)
        return pair_sums(plan, place, info, mix, pieces, nx, slots, env_rows)

    sums = {}
    for e in reversed(range(half_z)):
        keep, *away = partial_sums(e)
        for f, value in enumerate(away):
            keep = keep + send(value, lambda x, c, z, y, f=f: (x ^ (f + 1), c, z, y)).astype(F32)
        sums[e] = keep
    bit = 1
    while bit < half_z:
        for e in [e for e in sums if e & bit]:
            got = send(sums.pop(e).astype(BF16), lambda x, c, z, y: (x, c, z ^ bit, y))
            sums[e ^ bit] = sums[e ^ bit] + got.astype(F32)
        bit *= 2
    own = sums[0].reshape(2, nb, blk, blk)
    same = lax.dynamic_index_in_dim(own, c, 0, keepdims=False)
    other = lax.dynamic_index_in_dim(own, 1 - c, 0, keepdims=False)
    same16, other16 = same.astype(BF16), other.astype(BF16)

    def over_z(flip):
        def to(x, c, z, y):
            return (x, c ^ flip, z ^ half_z, y) if c != z // half_z else None

        return to

    got = send(same16, over_z(0)).astype(F32) + send(other16, over_z(1)).astype(F32)
    near = send(other16, lambda x, c, z, y: (x, 1 - c, z, y) if c == z // half_z else None)
    result = jnp.where(c == top, same, near.astype(F32)) + got
    return result[None]


def solution(mesh):
    return jax.shard_map(
        functools.partial(per_device, mesh.shape["sec"], mesh.shape["term"]),
        mesh=mesh,
        in_specs=(
            P("term", "sec", None, None),
            P("sec", "term", None),
            P(None, None, "sec"),
            P("sec"),
            P("sec"),
            P(),
        ),
        out_specs=P("term", "sec", None, None),
        check_vma=False,
    )
```

```python
import functools

import jax
import jax.numpy as jnp
from jax import lax
from jax.experimental import pallas as pl
from jax.experimental.pallas import tpu as pltpu
from jax.sharding import PartitionSpec as P

BF16, F32 = jnp.bfloat16, jnp.float32
TILE = 16
VMEM_LIMIT = 48 << 20


def mix_kernel(count, flip, weights, *refs):
    envs, outs = refs[:count], refs[count:]
    nb, blk = envs[0].shape[0], envs[0].shape[2]
    combos, depth = weights.shape
    pairs = combos // len(outs)
    wide = depth * TILE
    spread = (
        lax.broadcasted_iota(jnp.int32, (depth, wide), 0)
        == lax.broadcasted_iota(jnp.int32, (depth, wide), 1) // TILE
    )
    spread = jnp.where(spread, 1.0, 0.0).astype(BF16)
    rows = jnp.dot(weights[...], spread, preferred_element_type=F32)
    rows = jnp.broadcast_to(rows[:, None, :], (combos, TILE, wide)).reshape(combos * TILE, wide)
    same = lax.broadcasted_iota(jnp.int32, rows.shape, 0) % TILE == (
        lax.broadcasted_iota(jnp.int32, rows.shape, 1) % TILE
    )
    mix = jnp.where(same, rows, 0.0).astype(BF16)
    order = lax.broadcasted_iota(jnp.int32, (blk, blk), 0) == (
        lax.broadcasted_iota(jnp.int32, (blk, blk), 1) ^ flip[0]
    )
    order = jnp.where(order, 1.0, 0.0).astype(BF16)

    def some_rows(step, carry):
        at = pl.multiple_of(((step * TILE) ^ flip[0]) // TILE * TILE, TILE)
        env = jnp.concatenate(
            [ref[i, pl.ds(at, TILE), :] for ref in envs for i in range(nb)], axis=0
        )
        env = jnp.dot(env, order, preferred_element_type=F32).astype(BF16)
        to = pl.multiple_of(step * TILE, TILE)
        for n, out in enumerate(outs):
            part = mix[n * pairs * TILE : (n + 1) * pairs * TILE]
            got = jnp.dot(part, env, preferred_element_type=F32).astype(BF16)
            out[:, pl.ds(to, TILE), :] = got.reshape(pairs, TILE, blk)
        return carry

    lax.fori_loop(0, blk // TILE, some_rows, 0)


def pair_kernel(count, groups, info, flip, mixed, *refs):
    halves = (refs[:count], refs[count : 2 * count])
    outs = refs[2 * count : -1]
    total = refs[-1]
    pairs, blk = mixed.shape[0], mixed.shape[1]
    total[...] = jnp.zeros_like(total)
    row = lax.broadcasted_iota(jnp.int32, (blk, blk), 0) ^ flip[0]
    col = lax.broadcasted_iota(jnp.int32, (blk, blk), 1)
    for n, half_refs in enumerate(halves):

        def one_pair(q, carry, half_refs=half_refs, first=n * (pairs // 2)):
            p = first + q
            keep = (row < info[0, p]) & (col < info[1, p])
            core = jnp.concatenate([ref[q].astype(F32) for ref in half_refs], axis=0)
            masked = jnp.where(keep, core, 0.0).astype(BF16)
            half = jnp.dot(mixed[p], masked, preferred_element_type=F32).astype(BF16)
            term = lax.dot_general(
                masked, half, (((0,), (0,)), ((), ())), preferred_element_type=F32
            )
            total[info[2, p]] += term
            return carry

        lax.fori_loop(0, pairs // 2, one_pair, 0, unroll=4)
    size = total.shape[0] // len(outs)
    for f, ref in enumerate(outs):
        ref[...] = total[f * size : (f + 1) * size].astype(ref.dtype)


SMEM = pl.BlockSpec(memory_space=pltpu.SMEM)
VMEM = pl.BlockSpec(memory_space=pltpu.VMEM)


def mix_envs(flip, weights, envs, terms):
    combos, depth = weights.shape
    blk = envs[0].shape[2]
    macs = combos * depth * TILE * blk * blk
    return pl.pallas_call(
        functools.partial(mix_kernel, len(envs)),
        out_shape=[jax.ShapeDtypeStruct((combos // terms, blk, blk), BF16)] * terms,
        in_specs=[SMEM] + [VMEM] * (1 + len(envs)),
        out_specs=[VMEM] * terms,
        compiler_params=pltpu.CompilerParams(vmem_limit_bytes=VMEM_LIMIT),
        cost_estimate=pl.CostEstimate(flops=2 * macs, bytes_accessed=10 << 20, transcendentals=0),
        name="mix_envs",
    )(flip, weights, *envs)


def pair_sums(info, flip, mixed, own, others, groups, nb):
    pairs, blk = mixed.shape[:2]
    macs = 2 * pairs * blk * blk * blk
    return pl.pallas_call(
        functools.partial(pair_kernel, len(own), groups),
        out_shape=[jax.ShapeDtypeStruct((nb, blk, blk), F32)] * 2
        + [jax.ShapeDtypeStruct((nb, blk, blk), BF16)] * (2 * groups - 2),
        in_specs=[SMEM, SMEM] + [VMEM] * (1 + len(own) + len(others)),
        out_specs=[VMEM] * (2 * groups),
        scratch_shapes=[pltpu.VMEM((2 * groups * nb, blk, blk), F32)],
        compiler_params=pltpu.CompilerParams(vmem_limit_bytes=VMEM_LIMIT),
        cost_estimate=pl.CostEstimate(flops=2 * macs, bytes_accessed=10 << 20, transcendentals=0),
        name="pair_sums",
    )(info, flip, mixed, *own, *others)


def per_device(secs, terms, env_blocks, core_blocks, mpo_coeffs, pair_left, pair_right, block_dims):
    nx, nz = secs // 2, terms // 2
    half_z = nz // 2
    nb, blk = env_blocks.shape[1], env_blocks.shape[2]
    pairs_local, rows = core_blocks.shape[0], core_blocks.shape[1]
    piece_pairs = pairs_local // nz
    sec, term = lax.axis_index("sec"), lax.axis_index("term")
    x, c, z, y = sec // 2, sec % 2, term // 2, term % 2
    top, rest = z // half_z, z % half_z

    def send(value, to):
        perm = []
        for s in range(secs):
            for t in range(terms):
                d = to(s // 2, s % 2, t // 2, t % 2)
                if d is not None and d != (s // 2, s % 2, t // 2, t % 2):
                    perm.append((s * terms + t, (d[0] * 2 + d[1]) * terms + d[2] * 2 + d[3]))
        return lax.ppermute(value, ("sec", "term"), perm)

    def other_core(value):
        return send(value, lambda x, c, z, y: (x, 1 - c, z, y))

    def other_y(value):
        return send(value, lambda x, c, z, y: (x, c, z, 1 - y))

    envs = [
        jnp.where(
            c == top,
            env_blocks[0],
            send(
                env_blocks[0],
                lambda x, c, z, y: (x, 1 - c, z ^ half_z, y) if c != z // half_z else None,
            ),
        )
    ]
    near = z ^ jnp.where(c == top, 0, half_z)
    from_z, from_y = [0], [0]
    bit = 1
    while bit < half_z:
        envs += [send(v, lambda x, c, z, y: (x, c, z ^ bit, y)) for v in envs]
        from_z += [a ^ bit for a in from_z]
        bit *= 2
    envs += [other_y(v) for v in envs]
    from_y = [0] * len(from_z) + [1] * len(from_z)
    from_z = from_z * 2
    envs += [other_core(v) for v in envs]
    from_y = from_y * 2
    from_z = from_z + [a ^ half_z for a in from_z]
    env_terms = jnp.stack([2 * (near ^ a) + (y ^ b) for a, b in zip(from_z, from_y)])

    own, others = [], []
    for m in range(nz):
        g = z ^ m
        piece = lax.dynamic_slice_in_dim(core_blocks, g * piece_pairs, piece_pairs, 0)
        got = send(
            piece,
            lambda x, c, z, y, m=m: (x, (z ^ m) % 2, c * half_z + (z ^ m) // 2, y),
        )
        stays = (c == g % 2) & (z == c * half_z + g // 2)
        own.append(jnp.where(stays, piece, got))
    own = [[v, other_y(v)] for v in own]
    flip = (2 * rest + c) * 2 * rows
    if rows % TILE == 0:
        flip = flip + y * rows
    else:
        own = [[jnp.where(y == 0, jnp.concatenate(v, 1), jnp.concatenate(v[::-1], 1))] for v in own]
    others = [[other_core(v) for v in pair] for pair in own]
    others = [others[m ^ 1] for m in range(nz)]
    own = [v for pair in own for v in pair]
    others = [v for pair in others for v in pair]
    flip = flip[None].astype(jnp.int32)

    facts = jnp.concatenate(
        [
            mpo_coeffs.reshape(-1, pairs_local).astype(F32),
            pair_left[None].astype(F32),
            pair_right[None].astype(F32),
        ]
    )
    facts = jnp.where(c == top, facts, other_core(facts))
    facts = jnp.concatenate(
        [
            lax.dynamic_slice_in_dim(facts, (2 * rest + k) * piece_pairs, piece_pairs, 1)
            for k in (c, 1 - c)
        ],
        axis=1,
    )
    left, right = facts[-2].astype(jnp.int32), facts[-1].astype(jnp.int32)
    coeffs = facts[:-2].reshape(mpo_coeffs.shape[0], mpo_coeffs.shape[1], -1)
    ids = jnp.arange(block_dims.shape[0])
    left_block = (x * 2 + top) * nb + left
    dims_left = jnp.sum(jnp.where(left_block[:, None] == ids, block_dims, 0), axis=1)
    dims_right = jnp.sum(jnp.where(right[:, None] == ids, block_dims, 0), axis=1)
    to_sec, to_block = right // nb, right % nb
    slot = (((to_sec // 2) ^ x) * 2 + ((to_sec % 2) ^ top)) * nb + to_block
    info = jnp.stack([dims_left, dims_right, slot])

    mine = jnp.stack([2 * (c * half_z + (rest ^ t)) + y for t in range(half_z)])
    pick_w = (env_terms[:, None] == jnp.arange(mpo_coeffs.shape[0])).astype(BF16)
    pick_v = (mine[:, None] == jnp.arange(mpo_coeffs.shape[1])).astype(BF16)
    weights = jnp.einsum("nw,wvp->nvp", pick_w, coeffs.astype(BF16), preferred_element_type=F32)
    weights = jnp.einsum("tv,nvp->tpn", pick_v, weights.astype(BF16), preferred_element_type=F32)
    onehot = left[:, None] == jnp.arange(nb)
    weights = jnp.where(onehot[None, :, None, :], weights[..., None], 0.0).astype(BF16)
    weights = weights.reshape(half_z * left.shape[0], -1)
    mixed = mix_envs(flip, weights, envs, half_z)

    result = None
    for t in reversed(range(half_z)):
        parts = pair_sums(info, flip, mixed[t], own, others, nx, nb)
        for b in range(2):
            part = parts[b]
            for f in range(1, nx):
                got = send(parts[2 * f + b], lambda x, c, z, y: (x ^ f, c, z, y))
                part = part + got.astype(F32)
            got = send(
                part.astype(BF16),
                lambda x, c, z, y: (x, (z // half_z) ^ b, c * half_z + ((z % half_z) ^ t), y),
            ).astype(F32)
            if t == 0 and b == 0:
                got = got + jnp.where(c == top, part, 0.0)
            result = got if result is None else result + got
    return result[None]


def solution(mesh):
    return jax.shard_map(
        functools.partial(per_device, mesh.shape["sec"], mesh.shape["term"]),
        mesh=mesh,
        in_specs=(
            P("term", "sec", None, None),
            P("sec", "term", None),
            P(None, None, "sec"),
            P("sec"),
            P("sec"),
            P(),
        ),
        out_specs=P("term", "sec", None, None),
        check_vma=False,
    )
```

```python
import functools

import jax
import jax.numpy as jnp
from jax import lax
from jax.experimental import pallas as pl
from jax.experimental.pallas import tpu as pltpu
from jax.sharding import PartitionSpec as P

BF16, F32 = jnp.bfloat16, jnp.float32
TILE = 16
VMEM_LIMIT = 16 << 20


def mix_kernel(count, flip, dims, weights, *refs):
    envs, outs = refs[:count], refs[count:-2]
    mix, ordered = refs[-2:]
    nb, blk = envs[0].shape[0], envs[0].shape[2]
    combos, depth = weights.shape
    pairs = combos // len(outs)
    wide = depth * TILE
    spread = (
        lax.broadcasted_iota(jnp.int32, (depth, wide), 0)
        == lax.broadcasted_iota(jnp.int32, (depth, wide), 1) // TILE
    )
    spread = jnp.where(spread, 1.0, 0.0).astype(BF16)
    rows = jnp.dot(weights[...], spread, preferred_element_type=F32)
    rows = jnp.broadcast_to(rows[:, None, :], (combos, TILE, wide)).reshape(combos * TILE, wide)
    same = lax.broadcasted_iota(jnp.int32, rows.shape, 0) % TILE == (
        lax.broadcasted_iota(jnp.int32, rows.shape, 1) % TILE
    )
    mix[...] = jnp.where(same, rows, 0.0).astype(BF16)
    order = lax.broadcasted_iota(jnp.int32, (blk, blk), 0) == (
        lax.broadcasted_iota(jnp.int32, (blk, blk), 1) ^ flip[0]
    )
    order = jnp.where(order, 1.0, 0.0).astype(BF16)

    row = lax.broadcasted_iota(jnp.int32, (TILE, blk), 0)
    col = lax.broadcasted_iota(jnp.int32, (TILE, blk), 1)

    def order_rows(step, carry):
        at = pl.multiple_of(((step * TILE) ^ flip[0]) // TILE * TILE, TILE)
        used = [
            jnp.where((row + at < dims[i]) & (col < dims[i]), 1.0, 0.0).astype(BF16)
            for i in range(nb)
        ]
        env = jnp.concatenate(
            [ref[i, pl.ds(at, TILE), :] * used[i] for ref in envs for i in range(nb)], axis=0
        )
        ordered[step] = jnp.dot(env, order, preferred_element_type=F32).astype(BF16)
        return carry

    lax.fori_loop(0, blk // TILE, order_rows, 0, unroll=True)

    def mix_rows(step, carry):
        to = pl.multiple_of(step * TILE, TILE)
        for n, out in enumerate(outs):
            part = mix[n * pairs * TILE : (n + 1) * pairs * TILE, :]
            got = jnp.dot(part, ordered[step], preferred_element_type=F32).astype(BF16)
            out[:, pl.ds(to, TILE), :] = got.reshape(pairs, TILE, blk)
        return carry

    lax.fori_loop(0, blk // TILE, mix_rows, 0, unroll=True)


def pair_kernel(count, slots, dims, mixed, *refs):
    halves = (refs[:count], refs[count : 2 * count])
    outs = refs[2 * count : -1]
    total = refs[-1]
    pairs, blk = mixed.shape[0], mixed.shape[1]
    total[...] = jnp.zeros_like(total)
    for n, half_refs in enumerate(halves):

        def one_pair(q, carry, half_refs=half_refs, first=n * (pairs // 2)):
            p = first + q
            core = jnp.concatenate([ref[q] for ref in half_refs], axis=0)
            half = jnp.dot(mixed[p], core, preferred_element_type=F32).astype(BF16)
            term = lax.dot_general(
                core, half, (((0,), (0,)), ((), ())), preferred_element_type=F32
            )
            total[slots[p]] += term
            return carry

        lax.fori_loop(0, pairs // 2, one_pair, 0, unroll=True)
    row = lax.broadcasted_iota(jnp.int32, (blk, blk), 0)
    col = lax.broadcasted_iota(jnp.int32, (blk, blk), 1)
    size = total.shape[0] // len(outs)
    for f, ref in enumerate(outs):
        for i in range(size):
            s = f * size + i
            keep = (row < dims[s]) & (col < dims[s])
            ref[i] = jnp.where(keep, total[s], 0.0).astype(ref.dtype)


SMEM = pl.BlockSpec(memory_space=pltpu.SMEM)
VMEM = pl.BlockSpec(memory_space=pltpu.VMEM)


def mix_envs(flip, dims, weights, envs, terms):
    combos, depth = weights.shape
    blk = envs[0].shape[2]
    macs = combos * depth * TILE * blk * blk
    return pl.pallas_call(
        functools.partial(mix_kernel, len(envs)),
        out_shape=[jax.ShapeDtypeStruct((combos // terms, blk, blk), BF16)] * terms,
        in_specs=[SMEM, SMEM] + [VMEM] * (1 + len(envs)),
        out_specs=[VMEM] * terms,
        scratch_shapes=[
            pltpu.VMEM((combos * TILE, depth * TILE), BF16),
            pltpu.VMEM((blk // TILE, depth * TILE, blk), BF16),
        ],
        compiler_params=pltpu.CompilerParams(vmem_limit_bytes=VMEM_LIMIT),
        cost_estimate=pl.CostEstimate(flops=2 * macs, bytes_accessed=10 << 20, transcendentals=0),
        name="mix_envs",
    )(flip, dims, weights, *envs)


def pair_sums(slots, dims, mixed, own, others, groups, nb):
    pairs, blk = mixed.shape[:2]
    macs = 2 * pairs * blk * blk * blk
    return pl.pallas_call(
        functools.partial(pair_kernel, len(own)),
        out_shape=[jax.ShapeDtypeStruct((nb, blk, blk), F32)] * 2
        + [jax.ShapeDtypeStruct((nb, blk, blk), BF16)] * (2 * groups - 2),
        in_specs=[SMEM, SMEM] + [VMEM] * (1 + len(own) + len(others)),
        out_specs=[VMEM] * (2 * groups),
        scratch_shapes=[pltpu.VMEM((2 * groups * nb, blk, blk), F32)],
        compiler_params=pltpu.CompilerParams(vmem_limit_bytes=VMEM_LIMIT),
        cost_estimate=pl.CostEstimate(flops=2 * macs, bytes_accessed=10 << 20, transcendentals=0),
        name="pair_sums",
    )(slots, dims, mixed, *own, *others)


def per_device(secs, terms, env_blocks, core_blocks, mpo_coeffs, pair_left, pair_right, block_dims):
    nx, nz = secs // 2, terms // 2
    half_z = nz // 2
    nb, blk = env_blocks.shape[1], env_blocks.shape[2]
    pairs_local, rows = core_blocks.shape[0], core_blocks.shape[1]
    piece_pairs = pairs_local // nz
    sec, term = lax.axis_index("sec"), lax.axis_index("term")
    x, c, z, y = sec // 2, sec % 2, term // 2, term % 2
    top, rest = z // half_z, z % half_z

    def send(value, to):
        perm = []
        for s in range(secs):
            for t in range(terms):
                d = to(s // 2, s % 2, t // 2, t % 2)
                if d is not None and d != (s // 2, s % 2, t // 2, t % 2):
                    perm.append((s * terms + t, (d[0] * 2 + d[1]) * terms + d[2] * 2 + d[3]))
        return lax.ppermute(value, ("sec", "term"), perm)

    def other_core(value):
        return send(value, lambda x, c, z, y: (x, 1 - c, z, y))

    def other_y(value):
        return send(value, lambda x, c, z, y: (x, c, z, 1 - y))

    facts = jnp.concatenate(
        [
            mpo_coeffs.reshape(-1, pairs_local).astype(F32),
            pair_left[None].astype(F32),
            pair_right[None].astype(F32),
        ]
    )

    parts = core_blocks.reshape(half_z, 2, piece_pairs, rows, blk)
    keep = lax.dynamic_index_in_dim(parts, c, 1, keepdims=False)
    got = other_core(lax.dynamic_index_in_dim(parts, 1 - c, 1, keepdims=False))
    pieces = []
    for d in range(nz):
        to = z ^ d
        mine, theirs = (
            lax.dynamic_index_in_dim(v, to % half_z, 0, keepdims=False) for v in (keep, got)
        )
        pieces.append(jnp.where(to // half_z == c, mine, theirs))
    got = send(
        env_blocks[0],
        lambda x, c, z, y: (x, 1 - c, z ^ half_z, y) if c != z // half_z else None,
    )
    early = [send(v, lambda x, c, z, y: (x, c, z ^ d, y)) if d else v for d, v in enumerate(pieces)]
    late = [other_y(v) for v in early]

    got, late[0] = lax.optimization_barrier((got, late[0]))
    envs = [jnp.where(c == top, env_blocks[0], got)]
    near = z ^ jnp.where(c == top, 0, half_z)
    from_z, from_y = [0], [0]
    bit = 1
    while bit < half_z:
        envs += [send(v, lambda x, c, z, y: (x, c, z ^ bit, y)) for v in envs]
        from_z += [a ^ bit for a in from_z]
        bit *= 2
    envs += [other_y(v) for v in envs]
    from_y = [0] * len(from_z) + [1] * len(from_z)
    from_z = from_z * 2
    envs += [other_core(v) for v in envs]
    from_y = from_y * 2
    from_z = from_z + [a ^ half_z for a in from_z]
    env_terms = jnp.stack([2 * (near ^ a) + (y ^ b) for a, b in zip(from_z, from_y)])

    facts = jnp.where(c == top, facts, other_core(facts))
    facts = jnp.concatenate(
        [
            lax.dynamic_slice_in_dim(facts, (2 * rest + k) * piece_pairs, piece_pairs, 1)
            for k in (c, 1 - c)
        ],
        axis=1,
    )
    left, right = facts[-2].astype(jnp.int32), facts[-1].astype(jnp.int32)
    coeffs = facts[:-2].reshape(mpo_coeffs.shape[0], mpo_coeffs.shape[1], -1)
    ids = jnp.arange(block_dims.shape[0])
    left_dims = jnp.sum(
        jnp.where(((x * 2 + top) * nb + jnp.arange(nb))[:, None] == ids, block_dims, 0), axis=1
    )
    to_sec, to_block = right // nb, right % nb
    slots = (((to_sec // 2) ^ x) * 2 + ((to_sec % 2) ^ top)) * nb + to_block
    places = jnp.arange(secs * nb)
    slot_sec = ((places // (2 * nb)) ^ x) * 2 + ((places // nb % 2) ^ top)
    slot_dims = jnp.sum(
        jnp.where((slot_sec * nb + places % nb)[:, None] == ids, block_dims, 0), axis=1
    )

    mine = jnp.stack([2 * (c * half_z + (rest ^ t)) + y for t in range(half_z)])
    pick_w = (env_terms[:, None] == jnp.arange(mpo_coeffs.shape[0])).astype(BF16)
    pick_v = (mine[:, None] == jnp.arange(mpo_coeffs.shape[1])).astype(BF16)
    weights = jnp.einsum("nw,wvp->nvp", pick_w, coeffs.astype(BF16), preferred_element_type=F32)
    weights = jnp.einsum("tv,nvp->tpn", pick_v, weights.astype(BF16), preferred_element_type=F32)
    onehot = left[:, None] == jnp.arange(nb)
    weights = jnp.where(onehot[None, :, None, :], weights[..., None], 0.0).astype(BF16)
    weights = weights.reshape(half_z * left.shape[0], -1)
    flip = z * 2 * rows + (y * rows if rows % TILE == 0 else 0)
    flip = flip[None].astype(jnp.int32)
    mixed = mix_envs(flip, left_dims, weights, envs, half_z)

    early = lax.optimization_barrier(tuple(early))
    early_others = [other_core(v) for v in early]
    late, early_others = lax.optimization_barrier((late, early_others))
    late_others = [other_core(v) for v in late]
    own = list(zip(early, late))
    others = list(zip(early_others, late_others))
    if rows % TILE:
        own, others = (
            [[jnp.where(y == 0, jnp.concatenate(v, 1), jnp.concatenate(v[::-1], 1))] for v in group]
            for group in (own, others)
        )
    own = [v for pair in own for v in pair]
    others = [v for pair in others for v in pair]

    sums = {}
    for t in reversed(range(half_z)):
        parts = pair_sums(slots, slot_dims, mixed[t], own, others, nx, nb)
        for b in range(2):
            part = parts[b]
            for f in range(1, nx):
                got = send(parts[2 * f + b], lambda x, c, z, y: (x ^ f, c, z, y))
                part = part + got.astype(F32)
            sums[t, b] = part
    bit = 1
    while bit < half_z:
        for t, b in [at for at in sums if at[0] & bit]:
            got = send(sums.pop((t, b)).astype(BF16), lambda x, c, z, y: (x, c, z ^ bit, y))
            sums[t ^ bit, b] = sums[t ^ bit, b] + got.astype(F32)
        bit *= 2
    result = jnp.where(c == top, sums[0, 0], 0.0)
    for b in range(2):
        got = send(
            sums[0, b].astype(BF16),
            lambda x, c, z, y: (x, (z // half_z) ^ b, c * half_z + z % half_z, y),
        )
        result = result + got.astype(F32)
    return result[None]


def solution(mesh):
    return jax.shard_map(
        functools.partial(per_device, mesh.shape["sec"], mesh.shape["term"]),
        mesh=mesh,
        in_specs=(
            P("term", "sec", None, None),
            P("sec", "term", None),
            P(None, None, "sec"),
            P("sec"),
            P("sec"),
            P(),
        ),
        out_specs=P("term", "sec", None, None),
        check_vma=False,
    )
```

```python
import functools

import jax
import jax.numpy as jnp
from jax import lax
from jax.experimental import pallas as pl
from jax.experimental.pallas import tpu as pltpu
from jax.sharding import PartitionSpec as P

BF16, F32 = jnp.bfloat16, jnp.float32
TILE = 16
VMEM_LIMIT = 16 << 20


def mix_kernel(count, flip, dims, weights, *refs):
    envs, outs = refs[:count], refs[count:-2]
    mix, ordered = refs[-2:]
    nb, blk = envs[0].shape[0], envs[0].shape[2]
    combos, depth = weights.shape
    pairs = combos // len(outs)
    wide = depth * TILE
    spread = (
        lax.broadcasted_iota(jnp.int32, (depth, wide), 0)
        == lax.broadcasted_iota(jnp.int32, (depth, wide), 1) // TILE
    )
    spread = jnp.where(spread, 1.0, 0.0).astype(BF16)
    rows = jnp.dot(weights[...], spread, preferred_element_type=F32)
    rows = jnp.broadcast_to(rows[:, None, :], (combos, TILE, wide)).reshape(combos * TILE, wide)
    same = lax.broadcasted_iota(jnp.int32, rows.shape, 0) % TILE == (
        lax.broadcasted_iota(jnp.int32, rows.shape, 1) % TILE
    )
    mix[...] = jnp.where(same, rows, 0.0).astype(BF16)
    order = lax.broadcasted_iota(jnp.int32, (blk, blk), 0) == (
        lax.broadcasted_iota(jnp.int32, (blk, blk), 1) ^ flip[0]
    )
    order = jnp.where(order, 1.0, 0.0).astype(BF16)

    row = lax.broadcasted_iota(jnp.int32, (TILE, blk), 0)
    col = lax.broadcasted_iota(jnp.int32, (TILE, blk), 1)

    def order_rows(step, carry):
        at = pl.multiple_of(((step * TILE) ^ flip[0]) // TILE * TILE, TILE)
        used = [
            jnp.where((row + at < dims[i]) & (col < dims[i]), 1.0, 0.0).astype(BF16)
            for i in range(nb)
        ]
        env = jnp.concatenate(
            [ref[i, pl.ds(at, TILE), :] * used[i] for ref in envs for i in range(nb)], axis=0
        )
        ordered[step] = jnp.dot(env, order, preferred_element_type=F32).astype(BF16)
        return carry

    lax.fori_loop(0, blk // TILE, order_rows, 0, unroll=True)

    def mix_rows(step, carry):
        to = pl.multiple_of(step * TILE, TILE)
        for n, out in enumerate(outs):
            part = mix[n * pairs * TILE : (n + 1) * pairs * TILE, :]
            got = jnp.dot(part, ordered[step], preferred_element_type=F32).astype(BF16)
            out[:, pl.ds(to, TILE), :] = got.reshape(pairs, TILE, blk)
        return carry

    lax.fori_loop(0, blk // TILE, mix_rows, 0, unroll=True)


def pair_kernel(count, slots, dims, mixed, *refs):
    halves = (refs[:count], refs[count : 2 * count])
    outs = refs[2 * count : -1]
    total = refs[-1]
    pairs, blk = mixed.shape[0], mixed.shape[1]
    total[...] = jnp.zeros_like(total)
    for n, half_refs in enumerate(halves):

        def one_pair(q, carry, half_refs=half_refs, first=n * (pairs // 2)):
            p = first + q
            core = jnp.concatenate([ref[q] for ref in half_refs], axis=0)
            half = jnp.dot(mixed[p], core, preferred_element_type=F32).astype(BF16)
            term = lax.dot_general(
                core, half, (((0,), (0,)), ((), ())), preferred_element_type=F32
            )
            total[slots[p]] += term
            return carry

        lax.fori_loop(0, pairs // 2, one_pair, 0, unroll=True)
    row = lax.broadcasted_iota(jnp.int32, (blk, blk), 0)
    col = lax.broadcasted_iota(jnp.int32, (blk, blk), 1)
    size = total.shape[0] // len(outs)
    for f, ref in enumerate(outs):
        for i in range(size):
            s = f * size + i
            keep = (row < dims[s]) & (col < dims[s])
            ref[i] = jnp.where(keep, total[s], 0.0).astype(ref.dtype)


SMEM = pl.BlockSpec(memory_space=pltpu.SMEM)
VMEM = pl.BlockSpec(memory_space=pltpu.VMEM)


def mix_envs(flip, dims, weights, envs, terms):
    combos, depth = weights.shape
    blk = envs[0].shape[2]
    macs = combos * depth * TILE * blk * blk
    return pl.pallas_call(
        functools.partial(mix_kernel, len(envs)),
        out_shape=[jax.ShapeDtypeStruct((combos // terms, blk, blk), BF16)] * terms,
        in_specs=[SMEM, SMEM] + [VMEM] * (1 + len(envs)),
        out_specs=[VMEM] * terms,
        scratch_shapes=[
            pltpu.VMEM((combos * TILE, depth * TILE), BF16),
            pltpu.VMEM((blk // TILE, depth * TILE, blk), BF16),
        ],
        compiler_params=pltpu.CompilerParams(vmem_limit_bytes=VMEM_LIMIT),
        cost_estimate=pl.CostEstimate(flops=2 * macs, bytes_accessed=10 << 20, transcendentals=0),
        name="mix_envs",
    )(flip, dims, weights, *envs)


def pair_sums(slots, dims, mixed, own, others, dtypes, nb):
    pairs, blk = mixed.shape[:2]
    macs = 2 * pairs * blk * blk * blk
    return pl.pallas_call(
        functools.partial(pair_kernel, len(own)),
        out_shape=[jax.ShapeDtypeStruct((nb, blk, blk), d) for d in dtypes],
        in_specs=[SMEM, SMEM] + [VMEM] * (1 + len(own) + len(others)),
        out_specs=[VMEM] * len(dtypes),
        scratch_shapes=[pltpu.VMEM((len(dtypes) * nb, blk, blk), F32)],
        compiler_params=pltpu.CompilerParams(vmem_limit_bytes=VMEM_LIMIT),
        cost_estimate=pl.CostEstimate(flops=2 * macs, bytes_accessed=10 << 20, transcendentals=0),
        name="pair_sums",
    )(slots, dims, mixed, *own, *others)


def per_device(secs, terms, env_blocks, core_blocks, mpo_coeffs, pair_left, pair_right, block_dims):
    nx, nz = secs // 2, terms // 2
    half_z = nz // 2
    nb, blk = env_blocks.shape[1], env_blocks.shape[2]
    pairs_local, rows = core_blocks.shape[0], core_blocks.shape[1]
    piece_pairs = pairs_local // nz
    sec, term = lax.axis_index("sec"), lax.axis_index("term")
    x, c, z, y = sec // 2, sec % 2, term // 2, term % 2
    top, rest = z // half_z, z % half_z

    def send(value, to):
        perm = []
        for s in range(secs):
            for t in range(terms):
                d = to(s // 2, s % 2, t // 2, t % 2)
                if d is not None and d != (s // 2, s % 2, t // 2, t % 2):
                    perm.append((s * terms + t, (d[0] * 2 + d[1]) * terms + d[2] * 2 + d[3]))
        return lax.ppermute(value, ("sec", "term"), perm)

    def other_core(value):
        return send(value, lambda x, c, z, y: (x, 1 - c, z, y))

    def other_y(value):
        return send(value, lambda x, c, z, y: (x, c, z, 1 - y))

    facts = jnp.concatenate(
        [
            mpo_coeffs.reshape(-1, pairs_local).astype(F32),
            pair_left[None].astype(F32),
            pair_right[None].astype(F32),
        ]
    )

    parts = core_blocks.reshape(half_z, 2, piece_pairs, rows, blk)
    keep = lax.dynamic_index_in_dim(parts, c, 1, keepdims=False)
    got = other_core(lax.dynamic_index_in_dim(parts, 1 - c, 1, keepdims=False))
    pieces = []
    for d in range(nz):
        to = z ^ d
        mine, theirs = (
            lax.dynamic_index_in_dim(v, to % half_z, 0, keepdims=False) for v in (keep, got)
        )
        pieces.append(jnp.where(to // half_z == c, mine, theirs))
    got = send(
        env_blocks[0],
        lambda x, c, z, y: (x, 1 - c, z ^ half_z, y) if c != z // half_z else None,
    )
    early = [send(v, lambda x, c, z, y: (x, c, z ^ d, y)) if d else v for d, v in enumerate(pieces)]
    late = [other_y(v) for v in early]

    got, late[0] = lax.optimization_barrier((got, late[0]))
    envs = [jnp.where(c == top, env_blocks[0], got)]
    near = z ^ jnp.where(c == top, 0, half_z)
    envs += [other_y(envs[0])]
    from_z, from_y = [0, 0], [0, 1]
    bit = 1
    while bit < half_z:
        envs += [send(v, lambda x, c, z, y: (x, c, z ^ bit, y)) for v in envs]
        from_z += [a ^ bit for a in from_z]
        from_y = from_y * 2
        bit *= 2
    envs += [other_core(v) for v in envs]
    from_y = from_y * 2
    from_z = from_z + [a ^ half_z for a in from_z]
    env_terms = jnp.stack([2 * (near ^ a) + (y ^ b) for a, b in zip(from_z, from_y)])

    facts = jnp.where(c == top, facts, other_core(facts))
    facts = jnp.concatenate(
        [
            lax.dynamic_slice_in_dim(facts, (2 * rest + k) * piece_pairs, piece_pairs, 1)
            for k in (c, 1 - c)
        ],
        axis=1,
    )
    left, right = facts[-2].astype(jnp.int32), facts[-1].astype(jnp.int32)
    coeffs = facts[:-2].reshape(mpo_coeffs.shape[0], mpo_coeffs.shape[1], -1)
    ids = jnp.arange(block_dims.shape[0])
    left_dims = jnp.sum(
        jnp.where(((x * 2 + top) * nb + jnp.arange(nb))[:, None] == ids, block_dims, 0), axis=1
    )
    to_sec, to_block = right // nb, right % nb
    slots = (((to_sec // 2) ^ x) * 2 + ((to_sec % 2) ^ top)) * nb + to_block
    places = jnp.arange(secs * nb)
    slot_sec = ((places // (2 * nb)) ^ x) * 2 + ((places // nb % 2) ^ top)
    slot_dims = jnp.sum(
        jnp.where((slot_sec * nb + places % nb)[:, None] == ids, block_dims, 0), axis=1
    )

    mine = jnp.stack([2 * (c * half_z + (rest ^ t)) + y for t in range(half_z)])
    pick_w = (env_terms[:, None] == jnp.arange(mpo_coeffs.shape[0])).astype(BF16)
    pick_v = (mine[:, None] == jnp.arange(mpo_coeffs.shape[1])).astype(BF16)
    weights = jnp.einsum("nw,wvp->nvp", pick_w, coeffs.astype(BF16), preferred_element_type=F32)
    weights = jnp.einsum("tv,nvp->tpn", pick_v, weights.astype(BF16), preferred_element_type=F32)
    onehot = left[:, None] == jnp.arange(nb)
    weights = jnp.where(onehot[None, :, None, :], weights[..., None], 0.0).astype(BF16)
    weights = weights.reshape(half_z * left.shape[0], -1)
    flip = z * 2 * rows + (y * rows if rows % TILE == 0 else 0)
    flip = flip[None].astype(jnp.int32)
    mixed = mix_envs(flip, left_dims, weights, envs, half_z)

    early = lax.optimization_barrier(tuple(early))
    early_others = [other_core(v) for v in early]
    late, early_others = lax.optimization_barrier((late, early_others))
    late_others = [other_core(v) for v in late]
    own = list(zip(early, late))
    others = list(zip(early_others, late_others))
    if rows % TILE:
        own, others = (
            [[jnp.where(y == 0, jnp.concatenate(v, 1), jnp.concatenate(v[::-1], 1))] for v in group]
            for group in (own, others)
        )
    own = [v for pair in own for v in pair]
    others = [v for pair in others for v in pair]

    def over_x(parts):
        kept = parts[0].astype(F32)
        for f in range(1, nx):
            got = send(parts[f].astype(BF16), lambda x, c, z, y: (x ^ f, c, z, y))
            kept = kept + got.astype(F32)
        return kept

    def over_halves(terms):
        terms, bit = dict(terms), 1
        while bit < half_z:
            for t in [t for t in terms if t & bit]:
                got = send(terms.pop(t).astype(BF16), lambda x, c, z, y: (x, c, z ^ bit, y))
                terms[t ^ bit] = terms[t ^ bit].astype(F32) + got.astype(F32)
            bit *= 2
        return terms[0]

    first, second = {}, {}
    for t in reversed(range(half_z)):
        dtypes = [F32, BF16 if t % 2 else F32] + [BF16, BF16 if t % 2 else F32] * (nx - 1)
        parts = pair_sums(slots, slot_dims, mixed[t], own, others, dtypes, nb)
        first[t] = over_x(parts[::2])
        second[t] = parts[1::2]
    sums = [
        over_halves(first),
        over_x([over_halves({t: v[f] for t, v in second.items()}) for f in range(nx)]),
    ]
    result = jnp.where(c == top, sums[0], 0.0)
    for b in range(2):
        got = send(
            sums[b].astype(BF16),
            lambda x, c, z, y: (x, (z // half_z) ^ b, c * half_z + z % half_z, y),
        )
        result = result + got.astype(F32)
    return result[None]


def solution(mesh):
    return jax.shard_map(
        functools.partial(per_device, mesh.shape["sec"], mesh.shape["term"]),
        mesh=mesh,
        in_specs=(
            P("term", "sec", None, None),
            P("sec", "term", None),
            P(None, None, "sec"),
            P("sec"),
            P("sec"),
            P(),
        ),
        out_specs=P("term", "sec", None, None),
        check_vma=False,
    )
```

```python
import functools

import jax
import jax.numpy as jnp
from jax import lax
from jax.experimental import pallas as pl
from jax.experimental.pallas import tpu as pltpu
from jax.sharding import PartitionSpec as P

BF16, F32 = jnp.bfloat16, jnp.float32
TILE = 16
VMEM_LIMIT = 16 << 20


def mix_kernel(count, flip, dims, weights, *refs):
    envs, outs = refs[:count], refs[count:-2]
    mix, ordered = refs[-2:]
    nb, blk = envs[0].shape[0], envs[0].shape[2]
    combos, depth = weights.shape
    pairs = combos // len(outs)
    wide = depth * TILE
    spread = (
        lax.broadcasted_iota(jnp.int32, (depth, wide), 0)
        == lax.broadcasted_iota(jnp.int32, (depth, wide), 1) // TILE
    )
    spread = jnp.where(spread, 1.0, 0.0).astype(BF16)
    rows = jnp.dot(weights[...], spread, preferred_element_type=F32)
    rows = jnp.broadcast_to(rows[:, None, :], (combos, TILE, wide)).reshape(combos * TILE, wide)
    same = lax.broadcasted_iota(jnp.int32, rows.shape, 0) % TILE == (
        lax.broadcasted_iota(jnp.int32, rows.shape, 1) % TILE
    )
    mix[...] = jnp.where(same, rows, 0.0).astype(BF16)
    order = lax.broadcasted_iota(jnp.int32, (blk, blk), 0) == (
        lax.broadcasted_iota(jnp.int32, (blk, blk), 1) ^ flip[0]
    )
    order = jnp.where(order, 1.0, 0.0).astype(BF16)

    row = lax.broadcasted_iota(jnp.int32, (TILE, blk), 0)
    col = lax.broadcasted_iota(jnp.int32, (TILE, blk), 1)

    def order_rows(step, carry):
        at = pl.multiple_of(((step * TILE) ^ flip[0]) // TILE * TILE, TILE)
        used = [
            jnp.where((row + at < dims[i]) & (col < dims[i]), 1.0, 0.0).astype(BF16)
            for i in range(nb)
        ]
        env = jnp.concatenate(
            [ref[i, pl.ds(at, TILE), :] * used[i] for ref in envs for i in range(nb)], axis=0
        )
        ordered[step] = jnp.dot(env, order, preferred_element_type=F32).astype(BF16)
        return carry

    lax.fori_loop(0, blk // TILE, order_rows, 0, unroll=True)

    def mix_rows(step, carry):
        to = pl.multiple_of(step * TILE, TILE)
        for n, out in enumerate(outs):
            part = mix[n * pairs * TILE : (n + 1) * pairs * TILE, :]
            got = jnp.dot(part, ordered[step], preferred_element_type=F32).astype(BF16)
            out[:, pl.ds(to, TILE), :] = got.reshape(pairs, TILE, blk)
        return carry

    lax.fori_loop(0, blk // TILE, mix_rows, 0, unroll=True)


def pair_kernel(count, slots, dims, mixed, *refs):
    halves = (refs[:count], refs[count : 2 * count])
    outs = refs[2 * count : -1]
    total = refs[-1]
    pairs, blk = mixed.shape[0], mixed.shape[1]
    total[...] = jnp.zeros_like(total)
    for n, half_refs in enumerate(halves):

        def one_pair(q, carry, half_refs=half_refs, first=n * (pairs // 2)):
            p = first + q
            core = jnp.concatenate([ref[q] for ref in half_refs], axis=0)
            half = jnp.dot(mixed[p], core, preferred_element_type=F32).astype(BF16)
            term = lax.dot_general(
                core, half, (((0,), (0,)), ((), ())), preferred_element_type=F32
            )
            total[slots[p]] += term
            return carry

        lax.fori_loop(0, pairs // 2, one_pair, 0, unroll=True)
    row = lax.broadcasted_iota(jnp.int32, (blk, blk), 0)
    col = lax.broadcasted_iota(jnp.int32, (blk, blk), 1)
    size = total.shape[0] // len(outs)
    for f, ref in enumerate(outs):
        for i in range(size):
            s = f * size + i
            keep = (row < dims[s]) & (col < dims[s])
            ref[i] = jnp.where(keep, total[s], 0.0).astype(ref.dtype)


SMEM = pl.BlockSpec(memory_space=pltpu.SMEM)
VMEM = pl.BlockSpec(memory_space=pltpu.VMEM)


def mix_envs(flip, dims, weights, envs, terms):
    combos, depth = weights.shape
    blk = envs[0].shape[2]
    macs = combos * depth * TILE * blk * blk
    return pl.pallas_call(
        functools.partial(mix_kernel, len(envs)),
        out_shape=[jax.ShapeDtypeStruct((combos // terms, blk, blk), BF16)] * terms,
        in_specs=[SMEM, SMEM] + [VMEM] * (1 + len(envs)),
        out_specs=[VMEM] * terms,
        scratch_shapes=[
            pltpu.VMEM((combos * TILE, depth * TILE), BF16),
            pltpu.VMEM((blk // TILE, depth * TILE, blk), BF16),
        ],
        compiler_params=pltpu.CompilerParams(vmem_limit_bytes=VMEM_LIMIT),
        cost_estimate=pl.CostEstimate(flops=2 * macs, bytes_accessed=10 << 20, transcendentals=0),
        name="mix_envs",
    )(flip, dims, weights, *envs)


def pair_sums(slots, dims, mixed, own, others, dtypes, nb):
    pairs, blk = mixed.shape[:2]
    macs = 2 * pairs * blk * blk * blk
    return pl.pallas_call(
        functools.partial(pair_kernel, len(own)),
        out_shape=[jax.ShapeDtypeStruct((nb, blk, blk), d) for d in dtypes],
        in_specs=[SMEM, SMEM] + [VMEM] * (1 + len(own) + len(others)),
        out_specs=[VMEM] * len(dtypes),
        scratch_shapes=[pltpu.VMEM((len(dtypes) * nb, blk, blk), F32)],
        compiler_params=pltpu.CompilerParams(vmem_limit_bytes=VMEM_LIMIT),
        cost_estimate=pl.CostEstimate(flops=2 * macs, bytes_accessed=10 << 20, transcendentals=0),
        name="pair_sums",
    )(slots, dims, mixed, *own, *others)


def per_device(secs, terms, env_blocks, core_blocks, mpo_coeffs, pair_left, pair_right, block_dims):
    nx, nz = secs // 2, terms // 2
    half_z = nz // 2
    nb, blk = env_blocks.shape[1], env_blocks.shape[2]
    pairs_local, rows = core_blocks.shape[0], core_blocks.shape[1]
    piece_pairs = pairs_local // nz
    sec, term = lax.axis_index("sec"), lax.axis_index("term")
    x, c, z, y = sec // 2, sec % 2, term // 2, term % 2
    top, rest = z // half_z, z % half_z

    def send(value, to):
        perm = []
        for s in range(secs):
            for t in range(terms):
                d = to(s // 2, s % 2, t // 2, t % 2)
                if d is not None and d != (s // 2, s % 2, t // 2, t % 2):
                    perm.append((s * terms + t, (d[0] * 2 + d[1]) * terms + d[2] * 2 + d[3]))
        return lax.ppermute(value, ("sec", "term"), perm)

    def other_core(value):
        return send(value, lambda x, c, z, y: (x, 1 - c, z, y))

    def other_y(value):
        return send(value, lambda x, c, z, y: (x, c, z, 1 - y))

    facts = jnp.concatenate(
        [
            mpo_coeffs.reshape(-1, pairs_local).astype(F32),
            pair_left[None].astype(F32),
            pair_right[None].astype(F32),
        ]
    )

    parts = core_blocks.reshape(half_z, 2, piece_pairs, rows, blk)
    keep = lax.dynamic_index_in_dim(parts, c, 1, keepdims=False)
    got = other_core(lax.dynamic_index_in_dim(parts, 1 - c, 1, keepdims=False))
    pieces = []
    for d in range(nz):
        to = z ^ d
        mine, theirs = (
            lax.dynamic_index_in_dim(v, to % half_z, 0, keepdims=False) for v in (keep, got)
        )
        pieces.append(jnp.where(to // half_z == c, mine, theirs))
    got = send(
        env_blocks[0],
        lambda x, c, z, y: (x, 1 - c, z ^ half_z, y) if c != z // half_z else None,
    )
    early = [send(v, lambda x, c, z, y: (x, c, z ^ d, y)) if d else v for d, v in enumerate(pieces)]
    late = [other_y(v) for v in early]

    got, late[0] = lax.optimization_barrier((got, late[0]))
    envs = [jnp.where(c == top, env_blocks[0], got)]
    near = z ^ jnp.where(c == top, 0, half_z)
    envs += [other_y(envs[0])]
    from_z, from_y = [0, 0], [0, 1]
    bit = 1
    while bit < half_z:
        envs += [send(v, lambda x, c, z, y: (x, c, z ^ bit, y)) for v in envs]
        from_z += [a ^ bit for a in from_z]
        from_y = from_y * 2
        bit *= 2
    envs += [other_core(v) for v in envs]
    from_y = from_y * 2
    from_z = from_z + [a ^ half_z for a in from_z]
    env_terms = jnp.stack([2 * (near ^ a) + (y ^ b) for a, b in zip(from_z, from_y)])

    facts = jnp.where(c == top, facts, other_core(facts))
    facts = jnp.concatenate(
        [
            lax.dynamic_slice_in_dim(facts, (2 * rest + k) * piece_pairs, piece_pairs, 1)
            for k in (c, 1 - c)
        ],
        axis=1,
    )
    left, right = facts[-2].astype(jnp.int32), facts[-1].astype(jnp.int32)
    coeffs = facts[:-2].reshape(mpo_coeffs.shape[0], mpo_coeffs.shape[1], -1)
    ids = jnp.arange(block_dims.shape[0])
    left_dims = jnp.sum(
        jnp.where(((x * 2 + top) * nb + jnp.arange(nb))[:, None] == ids, block_dims, 0), axis=1
    )
    to_sec, to_block = right // nb, right % nb
    slots = (((to_sec // 2) ^ x) * 2 + ((to_sec % 2) ^ top)) * nb + to_block
    places = jnp.arange(secs * nb)
    slot_sec = ((places // (2 * nb)) ^ x) * 2 + ((places // nb % 2) ^ top)
    slot_dims = jnp.sum(
        jnp.where((slot_sec * nb + places % nb)[:, None] == ids, block_dims, 0), axis=1
    )

    mine = jnp.stack([2 * (c * half_z + (rest ^ t)) + y for t in range(half_z)])
    pick_w = (env_terms[:, None] == jnp.arange(mpo_coeffs.shape[0])).astype(BF16)
    pick_v = (mine[:, None] == jnp.arange(mpo_coeffs.shape[1])).astype(BF16)
    weights = jnp.einsum("nw,wvp->nvp", pick_w, coeffs.astype(BF16), preferred_element_type=F32)
    weights = jnp.einsum("tv,nvp->tpn", pick_v, weights.astype(BF16), preferred_element_type=F32)
    onehot = left[:, None] == jnp.arange(nb)
    weights = jnp.where(onehot[None, :, None, :], weights[..., None], 0.0).astype(BF16)
    weights = weights.reshape(half_z * left.shape[0], -1)
    flip = z * 2 * rows + (y * rows if rows % TILE == 0 else 0)
    flip = flip[None].astype(jnp.int32)
    mixed = mix_envs(flip, left_dims, weights, envs, half_z)

    early = lax.optimization_barrier(tuple(early))
    early_others = [other_core(v) for v in early]
    late, early_others = lax.optimization_barrier((late, early_others))
    late_others = [other_core(v) for v in late]
    own = list(zip(early, late))
    others = list(zip(early_others, late_others))
    if rows % TILE:
        own, others = (
            [[jnp.where(y == 0, jnp.concatenate(v, 1), jnp.concatenate(v[::-1], 1))] for v in group]
            for group in (own, others)
        )
    own = [v for pair in own for v in pair]
    others = [v for pair in others for v in pair]

    def over_x(parts):
        kept = parts[0].astype(F32)
        for f in range(1, nx):
            got = send(parts[f].astype(BF16), lambda x, c, z, y: (x ^ f, c, z, y))
            kept = kept + got.astype(F32)
        return kept

    def over_halves(terms):
        terms, bit = dict(terms), 1
        while bit < half_z:
            for t in [t for t in terms if t & bit]:
                got = send(terms.pop(t).astype(BF16), lambda x, c, z, y: (x, c, z ^ bit, y))
                terms[t ^ bit] = terms[t ^ bit].astype(F32) + got.astype(F32)
            bit *= 2
        return terms[0]

    first, second = {}, {}
    for t in reversed(range(half_z)):
        odd = BF16 if t % 2 else F32
        dtypes = [odd, F32] + [odd, BF16] * (nx - 1)
        parts = pair_sums(slots, slot_dims, mixed[t], own, others, dtypes, nb)
        first[t] = over_x(parts[1::2])
        second[t] = parts[::2]
    sums = [over_halves({t: v[f] for t, v in second.items()}) for f in range(nx)]
    sums = [over_x(sums), over_halves(first)]
    result = jnp.where(c == top, sums[0], 0.0)
    for b in range(2):
        got = send(
            sums[b].astype(BF16),
            lambda x, c, z, y: (x, (z // half_z) ^ b, c * half_z + z % half_z, y),
        )
        result = result + got.astype(F32)
    return result[None]


def solution(mesh):
    return jax.shard_map(
        functools.partial(per_device, mesh.shape["sec"], mesh.shape["term"]),
        mesh=mesh,
        in_specs=(
            P("term", "sec", None, None),
            P("sec", "term", None),
            P(None, None, "sec"),
            P("sec"),
            P("sec"),
            P(),
        ),
        out_specs=P("term", "sec", None, None),
        check_vma=False,
    )
```
